768 devices in a mesh: dp: 192 (over z, y, core), expert: 4 (over x).
Axes of the slice: x: 4, y: 8, z: 12, core: 2. Of those that a mesh axis runs over, the one named last changes fastest.
Arguments:
- gate_pre: bfloat16 [49152, 1024], P('dp', 'expert'), may hold values from -6 to 6
- up_pre: bfloat16 [49152, 1024], P('dp', 'expert'), may hold values from -6 to 6
- out_grad: bfloat16 [49152, 3840], P('dp'), may hold values from -24 to 24
- route_weight: float32 [49152], P('dp'), may hold values from 0.05 to 0.6
- counts: int32 [192], P('dp'), may hold values from 32 to 256, as said below
- down_weight: bfloat16 [3840, 1024], P('dp', 'expert'), may hold values from -0.1875 to 0.1875
Outputs:
- gate_grad: bfloat16 [49152, 1024], P('dp', 'expert')
- up_grad: bfloat16 [49152, 1024], P('dp', 'expert')
- route_grad: float32 [49152], P('dp')
- down_grad: float32 [3840, 1024], P('dp', 'expert')
The draws below stay inside these ranges and needn't reach their ends.
Inputs may be any that keep to these rules, and one draw needn't show every extreme that they name: The live rows of data shard i are its first counts[i] slots; some shard is full and some holds the fewest.
All inputs are finite; a program needn't handle non-finite values.
Results may differ from the reference program's by a relative error of at most 0.007.
Values may be sent and summed in bfloat16 or wider, within the bound.
A program may use at most 32 MiB of HBM per device.

```python
import math
import jax
import jax.numpy as jnp
from jax import lax

D = 3840
FF = 1024
ROWS_DEV = 256
ROWS = 49152
N_DP = 192


def draw_counts(key, part):
    key = jax.random.fold_in(key, 7)
    lowest = ROWS_DEV // 8
    spread_size = ROWS_DEV - lowest
    drawn_raw = jax.random.randint(jax.random.fold_in(key, 1), (N_DP,), 0, spread_size + 1)
    counts = lowest + drawn_raw * drawn_raw // spread_size
    heavy_shard = jax.random.randint(jax.random.fold_in(key, 2), (), 0, N_DP)
    offset_draw = jax.random.randint(jax.random.fold_in(key, 3), (), 1, N_DP)
    light_shard = (heavy_shard + offset_draw) % N_DP
    counts = counts.at[heavy_shard].set(ROWS_DEV)
    counts = counts.at[light_shard].set(lowest)
    return counts.astype(jnp.int32)


def with_spikes(values, rng, source, target, shards_of, factor):
    owner, partner = [(jnp.arange(values.shape[axis_at]) // (values.shape[axis_at] // shards_of)).reshape([-1 if axis == axis_at else 1 for axis in range(values.ndim)]) for axis_at in (source, target)]
    chosen = jax.random.permutation(rng, shards_of)[partner]
    strong = (owner == chosen) | (owner == (partner + shards_of // 2) % shards_of)
    return jnp.where(strong, factor * values, values)


def block_levels(stream_key, extent, cuts, smallest, largest):
    def one(axis_at, blocks):
        heights = jax.random.uniform(jax.random.fold_in(jax.random.fold_in(stream_key, 6), axis_at), (blocks,), jnp.float32, smallest / len(cuts), largest / len(cuts))
        return jnp.repeat(jnp.exp(heights), extent[axis_at] // blocks).reshape((-1,) + (1,) * (len(extent) - axis_at - 1))

    factor_of = one(*cuts[0])
    for cut in cuts[1:]:
        factor_of = factor_of * one(*cut)
    return factor_of


def gaussian(stream_key, shape, deviation, most, shards=(), kind=jnp.bfloat16):
    result = deviation * jax.random.normal(stream_key, shape, jnp.float32)
    if shards:
        result = result * block_levels(stream_key, shape, shards, -0.22, 0.18)
    return jnp.clip(result, -most, most).astype(kind)


def bell_draw_with(stream_key, shape, width, bound, cuts, heavy, kind=jnp.bfloat16):
    result = width * jax.random.normal(stream_key, shape, jnp.float32)
    if cuts:
        result = result * block_levels(stream_key, shape, cuts, -0.22, 0.18)
    return jnp.clip(with_spikes(result, jax.random.fold_in(stream_key, 3), *heavy), -bound, bound).astype(kind)


def setup_inputs(seed: int = 0) -> dict:
    keys = jax.random.split(jax.random.key(seed), 7)
    return {
        "gate_pre": gaussian(keys[0], (ROWS, FF), 1.0, 6.0, ((0, 192), (1, 4))),
        "up_pre": gaussian(keys[1], (ROWS, FF), 1.0, 6.0, ((0, 192), (1, 4))),
        "out_grad": bell_draw_with(keys[2], (ROWS, D), 1.0, 24.0, ((0, 192),), (0, 1, 192, 6.0)),
        "route_weight": jnp.clip(jnp.exp(math.log(0.6) - 2.4849067 * jax.random.uniform(keys[3], (ROWS,), jnp.float32) ** block_levels(keys[3], (ROWS,), ((0, 192),), -0.2, 0.2)), 0.05, 0.6),
        "counts": draw_counts(jax.random.fold_in(keys[6], 71), 0),
        "down_weight": gaussian(keys[5], (D, FF), FF ** -0.5, 0.1875, ((0, 192), (1, 4))),
    }


def reference(gate_pre, up_pre, out_grad, route_weight, counts, down_weight):
    grad_norm = 1.0 / math.sqrt(ROWS)
    slot_index = jnp.arange(ROWS_DEV, dtype=jnp.int32)

    def shard_step(running, pieces):
        gate_rows, up_rows, grad_rows, weight_rows, shard_count = pieces
        live_mask = (slot_index < shard_count).astype(jnp.float32)
        row_scale = weight_rows * live_mask
        gate_wide = gate_rows.astype(jnp.float32)
        up_wide = up_rows.astype(jnp.float32)
        sigmoid_gate = jax.nn.sigmoid(gate_wide)
        activated = gate_wide * sigmoid_gate
        hidden = (activated * up_wide).astype(jnp.bfloat16)
        back_proj = jnp.dot(grad_rows, down_weight, preferred_element_type=jnp.float32)
        hid_grad = back_proj * row_scale[:, None]
        gate_grad = (hid_grad * up_wide * sigmoid_gate * (1.0 + gate_wide * (1.0 - sigmoid_gate))).astype(jnp.bfloat16)
        up_grad = (hid_grad * activated).astype(jnp.bfloat16)
        route_grad = lax.optimization_barrier(jnp.sum(hidden.astype(jnp.float32) * back_proj, axis=1)) * live_mask
        scaled = (grad_rows.astype(jnp.float32) * row_scale[:, None]).astype(jnp.bfloat16)
        running = running + jnp.dot(scaled.T, hidden, preferred_element_type=jnp.float32)
        return (running, (gate_grad, up_grad, route_grad))
    shaped = (gate_pre.reshape(N_DP, ROWS_DEV, FF), up_pre.reshape(N_DP, ROWS_DEV, FF), out_grad.reshape(N_DP, ROWS_DEV, D), route_weight.reshape(N_DP, ROWS_DEV), counts.astype(jnp.int32))
    running, results = lax.scan(shard_step, jnp.zeros((D, FF), jnp.float32), shaped)
    gate_grad, up_grad, route_grad = results
    return (gate_grad.reshape(ROWS, FF), up_grad.reshape(ROWS, FF), route_grad.reshape(ROWS), running * grad_norm)
```

```python
import math

import jax
import jax.numpy as jnp
from jax import lax
from jax.experimental import pallas as pl
from jax.experimental.pallas import tpu as pltpu
from jax.sharding import PartitionSpec as P

MESH = pl.DeviceIdType.MESH
F32, BF16 = jnp.float32, jnp.bfloat16


def kernel(
    gate_ref, up_ref, og_ref, weight_ref, counts_ref, w_ref,
    gate_out, up_out, route_out, down_out,
    wf, g0_send, g0_recv, far, ybuf, wh, p_own, p_send, p_recv, r1_send, r1_recv,
    t_own, r2_send, r2_recv, u_own, r3_recv, f_send, f_recv, x_send, x_recv,
    hid, gate_co, up_co,
    pair_s, pair_r, far_s, far_r, y_s, y_r, near_s, near_r, fwd_s, fwd_r,
    psum_s, psum_r, r1_s, r1_r, r2_s, r2_r, r3_s, r3_r, x_s, x_r,
):
    me, x = lax.axis_index("dp"), lax.axis_index("expert")
    z, y, c = me // 16, lax.rem(me // 2, 8), lax.rem(me, 2)
    zdiv, zmod = z // 3, lax.rem(z, 3)
    first = c == 0

    def at(dz=0, dy=0, dc=0):
        return {"dp": lax.rem(z + dz, 12) * 16 + lax.rem(y + dy, 8) * 2 + lax.rem(c + dc, 2)}

    def across(k):
        return {"expert": lax.rem(x + k, 4)}

    def send(src, dst, ssem, rsem, device):
        copy = pltpu.make_async_remote_copy(
            src_ref=src, dst_ref=dst, send_sem=ssem, recv_sem=rsem, device_id=device, device_id_type=MESH
        )
        copy.start()
        return copy

    barrier = pltpu.get_barrier_semaphore()
    partners = [at(dc=1)] + [at(dz=d) for d in (1, 11, 3, 6, 9)] + [at(dy=d) for d in range(1, 8)]
    partners += [across(k) for k in range(1, 4)]
    for device in partners:
        pl.semaphore_signal(barrier, inc=1, device_id=device, device_id_type=MESH)

    wf[...] = jnp.zeros_like(wf)
    wf[0:20, :] = w_ref[...].astype(F32)
    g0_recv[24:40, :] = jnp.zeros((16, 128), F32)
    g0_send[...] = jnp.where(first, wf[0:24, 128:256], wf[0:24, 0:128])
    pl.semaphore_wait(barrier, len(partners))
    pair = send(g0_send, g0_recv.at[pl.ds(0, 24)], pair_s.at[0], pair_r.at[0], at(dc=1))

    eye = lax.broadcasted_iota(jnp.int32, (256, 256), 0) == lax.broadcasted_iota(jnp.int32, (256, 256), 1)
    live_row = (lax.broadcasted_iota(jnp.int32, (1, 256), 1) < counts_ref[0]).astype(F32)
    scale_row = weight_ref[...] * live_row
    scale = jnp.sum(jnp.where(eye, jnp.broadcast_to(scale_row, (256, 256)), 0.0), axis=1, keepdims=True)

    pair.wait_recv()
    mine = jnp.where(first, wf[:, 0:128], wf[:, 128:256])
    other = g0_recv[...]
    block = jnp.where(first, mine + pltpu.roll(other, 20, 0), other + pltpu.roll(mine, 20, 0))
    far[zdiv] = jnp.concatenate([block, jnp.zeros((8, 128), F32)], axis=0).astype(BF16)
    fars = [send(far.at[zdiv], far.at[zdiv], far_s.at[k - 1], far_r.at[k - 1], at(dz=3 * k)) for k in (2, 1, 3)]

    gate, up = gate_ref[...].astype(F32), up_ref[...].astype(F32)
    sig = jax.nn.sigmoid(gate)
    act = gate * sig
    hid[...] = (act * up).astype(BF16)
    gate_co[...] = scale * up * sig * (1.0 + gate * (1.0 - sig))
    up_co[...] = scale * act

    psums = []
    for k in range(6):
        scaled = (og_ref[:, 640 * k : 640 * (k + 1)].astype(F32) * scale).astype(BF16)
        part = lax.dot_general(scaled, hid[...], (((0,), (0,)), ((), ())), preferred_element_type=F32)
        lo, hi = part[:, 0:128], part[:, 128:256]
        p_own[2 * k : 2 * k + 2] = jnp.where(first, lo, hi).reshape(2, 320, 128)
        p_send[2 * k : 2 * k + 2] = jnp.where(first, hi, lo).reshape(2, 320, 128).astype(BF16)
        chunk = pl.ds(2 * k, 2)
        psums.append(send(p_send.at[chunk], p_recv.at[chunk], psum_s.at[k], psum_r.at[k], at(dc=1)))

    for copy in fars:
        copy.wait_recv()
    ybuf[y] = jnp.concatenate([far[j].astype(F32)[0:40] for j in range(4)], axis=0).astype(BF16)
    ys = [send(ybuf.at[y], ybuf.at[y], y_s.at[d - 1], y_r.at[d - 1], at(dy=d)) for d in (4, 3, 5, 2, 6, 1, 7)]

    for copy in psums:
        copy.wait_recv()
    r1s = []
    for j in range(4):
        for side, step in enumerate((1, 11)):
            at_z = 3 * j + lax.rem(zmod + step, 3)
            r1_send[side, j] = (p_own[at_z] + p_recv[at_z].astype(F32)).astype(BF16)
            r1s.append(send(r1_send.at[side, j], r1_recv.at[side, j], r1_s.at[side, j], r1_r.at[side, j], at(dz=step)))

    for copy in ys:
        copy.wait_recv()
    for j in range(4):
        rows = [ybuf[i].astype(F32)[40 * j : 40 * j + 40] for i in range(8)]
        wh[c, zmod, j] = jnp.concatenate(rows, axis=0).astype(BF16)
    nears = [
        send(wh.at[c, zmod], wh.at[c, zmod], near_s.at[side], near_r.at[side], at(dz=step))
        for side, step in enumerate((1, 11))
    ]
    fwds = [send(wh.at[c, zmod], wh.at[c, zmod], fwd_s.at[0], fwd_r.at[0], at(dc=1))]

    for copy in r1s:
        copy.wait_recv()
    for j in range(4):
        at_z = 3 * j + zmod
        total = p_own[at_z] + p_recv[at_z].astype(F32) + (r1_recv[0, j].astype(F32) + r1_recv[1, j].astype(F32))
        for i in range(8):
            t_own[i, 40 * j : 40 * j + 40, :] = total[40 * i : 40 * i + 40]
    r2_send[...] = t_own[...].astype(BF16)
    r2s = [
        send(r2_send.at[lax.rem(y + d, 8)], r2_recv.at[d - 1], r2_s.at[d - 1], r2_r.at[d - 1], at(dy=d))
        for d in (4, 3, 5, 2, 6, 1, 7)
    ]

    for side in range(2):
        nears[side].wait_recv()
        m = lax.rem(zmod + 2 - side, 3)
        fwds.append(send(wh.at[c, m], wh.at[c, m], fwd_s.at[side + 1], fwd_r.at[side + 1], at(dc=1)))

    for copy in r2s:
        copy.wait_recv()
    total = t_own[y]
    for d in range(7):
        total = total + r2_recv[d].astype(F32)
    u_own[...] = total.reshape(4, 40, 128)
    r3s = [
        send(u_own.at[lax.rem(zdiv + k, 4)], r3_recv.at[k - 1], r3_s.at[k - 1], r3_r.at[k - 1], at(dz=3 * k))
        for k in (2, 1, 3)
    ]

    for copy in fwds:
        copy.wait_recv()
    proj = None
    for k in range(6):
        halves = []
        for h in range(2):
            blocks = [wh[h, b % 3, b // 3] for b in (2 * k, 2 * k + 1)]
            halves.append(jnp.concatenate(blocks, axis=0))
        term = jnp.dot(
            og_ref[:, 640 * k : 640 * (k + 1)], jnp.concatenate(halves, axis=1), preferred_element_type=F32
        )
        proj = term if proj is None else proj + term
    match = jnp.sum(hid[...].astype(F32) * proj, axis=1, keepdims=True)
    match_row = jnp.sum(jnp.where(eye, jnp.broadcast_to(match, (256, 256)), 0.0), axis=0, keepdims=True)
    x_send[...] = jnp.broadcast_to(match_row, (8, 256))
    xs = [send(x_send, x_recv.at[k - 1], x_s.at[k - 1], x_r.at[k - 1], across(k)) for k in (2, 1, 3)]
    gate_out[...] = (proj * gate_co[...]).astype(BF16)
    up_out[...] = (proj * up_co[...]).astype(BF16)

    for copy in r3s:
        copy.wait_recv()
    total = (u_own[zdiv] + r3_recv[0] + (r3_recv[1] + r3_recv[2])) * (1.0 / math.sqrt(49152))
    turned = pltpu.roll(total, 20, 0)
    f_send[...] = jnp.where(first, turned, total)[0:24]
    final = send(f_send, f_recv, pair_s.at[1], pair_r.at[1], at(dc=1))
    keep = jnp.where(first, total, turned)[0:24]
    final.wait_recv()
    got = f_recv[...]
    down_out[:, 0:128] = jnp.where(first, keep, got)[0:20]
    down_out[:, 128:256] = jnp.where(first, got, keep)[0:20]

    for copy in xs:
        copy.wait_recv()
    everyone = x_send[...] + x_recv[0] + (x_recv[1] + x_recv[2])
    route_out[...] = everyone[0:1] * live_row
    for copy in [pair, final] + fars + ys + nears + fwds + psums + r1s + r2s + r3s + xs:
        copy.wait_send()


def on_device(gate_pre, up_pre, out_grad, route_weight, counts, down_weight):
    vmem = pl.BlockSpec(memory_space=pltpu.VMEM)
    dma = pltpu.SemaphoreType.DMA
    gate_grad, up_grad, route_grad, down_grad = pl.pallas_call(
        kernel,
        out_shape=(
            jax.ShapeDtypeStruct((256, 256), BF16),
            jax.ShapeDtypeStruct((256, 256), BF16),
            jax.ShapeDtypeStruct((1, 256), F32),
            jax.ShapeDtypeStruct((20, 256), F32),
        ),
        in_specs=[vmem, vmem, vmem, vmem, pl.BlockSpec(memory_space=pltpu.SMEM), vmem],
        out_specs=(vmem, vmem, vmem, vmem),
        scratch_shapes=[
            pltpu.VMEM((40, 256), F32),
            pltpu.VMEM((24, 128), F32),
            pltpu.VMEM((40, 128), F32),
            pltpu.VMEM((4, 48, 128), BF16),
            pltpu.VMEM((8, 160, 128), BF16),
            pltpu.VMEM((2, 3, 4, 320, 128), BF16),
            pltpu.VMEM((12, 320, 128), F32),
            pltpu.VMEM((12, 320, 128), BF16),
            pltpu.VMEM((12, 320, 128), BF16),
            pltpu.VMEM((2, 4, 320, 128), BF16),
            pltpu.VMEM((2, 4, 320, 128), BF16),
            pltpu.VMEM((8, 160, 128), F32),
            pltpu.VMEM((8, 160, 128), BF16),
            pltpu.VMEM((7, 160, 128), BF16),
            pltpu.VMEM((4, 40, 128), F32),
            pltpu.VMEM((3, 40, 128), F32),
            pltpu.VMEM((24, 128), F32),
            pltpu.VMEM((24, 128), F32),
            pltpu.VMEM((8, 256), F32),
            pltpu.VMEM((3, 8, 256), F32),
            pltpu.VMEM((256, 256), BF16),
            pltpu.VMEM((256, 256), F32),
            pltpu.VMEM((256, 256), F32),
            dma((2,)), dma((2,)), dma((3,)), dma((3,)), dma((7,)), dma((7,)), dma((2,)), dma((2,)), dma((3,)), dma((3,)),
            dma((6,)), dma((6,)), dma((2, 4)), dma((2, 4)), dma((7,)), dma((7,)), dma((3,)), dma((3,)), dma((3,)), dma((3,)),
        ],
        compiler_params=pltpu.CompilerParams(
            collective_id=0, has_side_effects=True, vmem_limit_bytes=48 * 1024 * 1024
        ),
        cost_estimate=pl.CostEstimate(flops=1_006_632_960, bytes_accessed=3_000_000, transcendentals=65536),
    )(gate_pre, up_pre, out_grad, route_weight.reshape(1, 256), counts, down_weight)
    return (gate_grad, up_grad, route_grad.reshape(256), down_grad)


def solution(mesh):
    return jax.shard_map(
        on_device,
        mesh=mesh,
        in_specs=(
            P("dp", "expert"),
            P("dp", "expert"),
            P("dp", None),
            P("dp"),
            P("dp"),
            P("dp", "expert"),
        ),
        out_specs=(P("dp", "expert"), P("dp", "expert"), P("dp"), P("dp", "expert")),
        check_vma=False,
    )
```

```python
import math

import jax
import jax.numpy as jnp
from jax import lax
from jax.experimental import pallas as pl
from jax.experimental.pallas import tpu as pltpu
from jax.sharding import PartitionSpec as P

MESH = pl.DeviceIdType.MESH
F32, BF16 = jnp.float32, jnp.bfloat16


NEAR_FIRST = (0, 1, 7, 2, 6, 3, 5, 4)
FAR_FIRST = (4, 3, 5, 2, 6, 1, 7, 0)


def kernel(
    gate_hbm, up_hbm, og_hbm, weight_hbm, counts_hbm, w_hbm,
    gate_hbm_out, up_hbm_out, route_hbm_out, down_hbm_out,
    gate_out, up_out, route_out, down_out,
    gate_ref, up_ref, og_ref, weight_ref, counts_ref, w_ref,
    wf, g0_send, g0_recv, yb, wt, p_own, p_other, p_send, p_recv, r1_send, r1_recv,
    t_own, r2_send, r2_recv, u_own, r3_recv, f_send, f_recv, x_send, x_recv,
    hid, gate_co, up_co,
    in_s, out_s, pair_s, pair_r, far_s, far_r, y_s, y_r, near_s, near_r, fwd_s, fwd_r,
    psum_s, psum_r, r1_s, r1_r, r2_s, r2_r, r3_s, r3_r, x_s, x_r,
):
    me, x = lax.axis_index("dp"), lax.axis_index("expert")
    z, y, c = me // 16, lax.rem(me // 2, 8), lax.rem(me, 2)
    zdiv, zmod = z // 3, lax.rem(z, 3)
    first = c == 0

    def at(dz=0, dy=0, dc=0):
        return {"dp": lax.rem(z + dz, 12) * 16 + lax.rem(y + dy, 8) * 2 + lax.rem(c + dc, 2)}

    def across(k):
        return {"expert": lax.rem(x + k, 4)}

    def send(src, dst, ssem, rsem, device):
        copy = pltpu.make_async_remote_copy(
            src_ref=src, dst_ref=dst, send_sem=ssem, recv_sem=rsem, device_id=device, device_id_type=MESH
        )
        copy.start()
        return copy

    incoming = []
    for k, (src, dst) in enumerate((
        (w_hbm, w_ref), (counts_hbm, counts_ref), (weight_hbm, weight_ref),
        (gate_hbm, gate_ref), (up_hbm, up_ref), (og_hbm, og_ref),
    )):
        incoming.append(pltpu.make_async_copy(src, dst, in_s.at[k]))
        incoming[-1].start()
    barrier = pltpu.get_barrier_semaphore()
    partners = [at(dz=d) for d in (6, 3, 9)] + [at(dy=d) for d in (4, 3, 5, 2, 6, 1, 7)]
    partners += [at(dz=1), at(dz=11), at(dc=1)] + [across(k) for k in (2, 1, 3)]
    for device in partners:
        pl.semaphore_signal(barrier, inc=1, device_id=device, device_id_type=MESH)

    wf[...] = jnp.zeros_like(wf)
    g0_recv[24:40, :] = jnp.zeros((16, 128), F32)
    incoming[0].wait()
    wf[0:20, :] = w_ref[...].astype(F32)
    g0_send[...] = jnp.where(first, wf[0:24, 128:256], wf[0:24, 0:128])

    for k in range(1, 5):
        incoming[k].wait()
    eye = lax.broadcasted_iota(jnp.int32, (256, 256), 0) == lax.broadcasted_iota(jnp.int32, (256, 256), 1)
    live_row = (lax.broadcasted_iota(jnp.int32, (1, 256), 1) < counts_ref[...]).astype(F32)
    scale_row = weight_ref[...] * live_row
    scale = jnp.sum(jnp.where(eye, jnp.broadcast_to(scale_row, (256, 256)), 0.0), axis=1, keepdims=True)
    gate, up = gate_ref[...].astype(F32), up_ref[...].astype(F32)
    sig = jax.nn.sigmoid(gate)
    act = gate * sig
    hid[...] = (act * up).astype(BF16)
    gate_co[...] = scale * up * sig * (1.0 + gate * (1.0 - sig))
    up_co[...] = scale * act
    incoming[5].wait()

    def shares(ks):
        for k in ks:
            scaled = (og_ref[:, 640 * k : 640 * (k + 1)].astype(F32) * scale).astype(BF16)
            part = lax.dot_general(scaled, hid[...], (((0,), (0,)), ((), ())), preferred_element_type=F32)
            lo, hi = part[:, 0:128], part[:, 128:256]
            own, other = jnp.where(first, lo, hi), jnp.where(first, hi, lo)
            for b in (0, 1):
                m, j = (2 * k + b) % 3, (2 * k + b) // 3
                for i in range(8):
                    at_row = 320 * b + 40 * i
                    p_own[m, i, 40 * j : 40 * j + 40, :] = own[at_row : at_row + 40]
                    p_other[m, i, 40 * j : 40 * j + 40, :] = other[at_row : at_row + 40]

    shares(range(6))
    pl.semaphore_wait(barrier, len(partners))
    pair = send(g0_send, g0_recv.at[pl.ds(0, 24)], pair_s.at[0], pair_r.at[0], at(dc=1))
    pair.wait_recv()
    mine = jnp.where(first, wf[:, 0:128], wf[:, 128:256])
    other = g0_recv[...]
    block = jnp.where(first, mine + pltpu.roll(other, 20, 0), other + pltpu.roll(mine, 20, 0))
    yb[y, zdiv] = jnp.concatenate([block, jnp.zeros((8, 128), F32)], axis=0).astype(BF16)
    piece = yb.at[y, zdiv]
    fars = {k: send(piece, piece, far_s.at[k - 1], far_r.at[k - 1], at(dz=3 * k)) for k in (2, 1, 3)}
    ys = {}

    def along_y(k):
        piece = yb.at[y, lax.rem(zdiv + 4 - k, 4)]
        for d in NEAR_FIRST[1:]:
            ys[k, d] = send(piece, piece, y_s.at[k, d], y_r.at[k, d], at(dy=d))

    along_y(0)

    psums = []
    for k in (1, 2, 0):
        m = lax.rem(zmod + k, 3)
        p_send[m] = p_other[m].astype(BF16)
        psums.append(send(p_send.at[m], p_recv.at[m], psum_s.at[k], psum_r.at[k], at(dc=1)))

    r1s = {}
    psums[0].wait_recv()
    psums[1].wait_recv()
    for d in FAR_FIRST:
        i = lax.rem(y + d, 8)
        for side, step in enumerate((1, 11)):
            m = lax.rem(zmod + step, 3)
            r1_send[side, i] = (p_own[m, i] + p_recv[m, i].astype(F32)).astype(BF16)
            r1s[side, d] = send(
                r1_send.at[side, i], r1_recv.at[side, i], r1_s.at[side, d], r1_r.at[side, d], at(dz=step)
            )

    for k in (1, 3, 2):
        fars[k].wait_recv()
        along_y(k)
    nears, fwds = {}, []

    def forward(m, i, sem):
        piece = wt.at[c, m, i]
        fwds.append(send(piece, piece, fwd_s.at[sem], fwd_r.at[sem], at(dc=1)))

    psums[2].wait_recv()
    r2s = {}
    for n in range(8):
        d = NEAR_FIRST[n]
        if d:
            for k in range(4):
                ys[k, d].wait_recv()
        i = lax.rem(y + 8 - d, 8)
        wt[c, zmod, i] = jnp.concatenate([yb[i, j].astype(F32)[0:40] for j in range(4)], axis=0).astype(BF16)
        for side, step in enumerate((1, 11)):
            piece = wt.at[c, zmod, i]
            nears[side, d] = send(piece, piece, near_s.at[side, d], near_r.at[side, d], at(dz=step))
        forward(zmod, i, d)
        d = FAR_FIRST[n]
        r1s[0, d].wait_recv()
        r1s[1, d].wait_recv()
        i = lax.rem(y + d, 8)
        total = p_own[zmod, i] + p_recv[zmod, i].astype(F32)
        total = total + (r1_recv[0, i].astype(F32) + r1_recv[1, i].astype(F32))
        if d:
            r2_send[d - 1] = total.astype(BF16)
            r2s[d] = send(r2_send.at[d - 1], r2_recv.at[d - 1], r2_s.at[d - 1], r2_r.at[d - 1], at(dy=d))
        else:
            t_own[...] = total

    for n in range(8):
        d = NEAR_FIRST[n]
        i = lax.rem(y + 8 - d, 8)
        for side in range(2):
            nears[side, d].wait_recv()
            forward(lax.rem(zmod + 2 - side, 3), i, 8 * side + 8 + d)

    total = t_own[...]
    for d in NEAR_FIRST[1:]:
        r2s[d].wait_recv()
        total = total + r2_recv[d - 1].astype(F32)
    u_own[...] = total.reshape(4, 40, 128)
    r3s = [
        send(u_own.at[lax.rem(zdiv + k, 4)], r3_recv.at[k - 1], r3_s.at[k - 1], r3_r.at[k - 1], at(dz=3 * k))
        for k in (2, 1, 3)
    ]

    for copy in fwds:
        copy.wait_recv()
    proj = None
    for k in range(6):
        halves = []
        for h in range(2):
            rows = [
                wt[h, b % 3, i].astype(F32)[40 * (b // 3) : 40 * (b // 3) + 40] for b in (2 * k, 2 * k + 1) for i in range(8)
            ]
            halves.append(jnp.concatenate(rows, axis=0).astype(BF16))
        term = jnp.dot(
            og_ref[:, 640 * k : 640 * (k + 1)], jnp.concatenate(halves, axis=1), preferred_element_type=F32
        )
        proj = term if proj is None else proj + term
    match = jnp.sum(hid[...].astype(F32) * proj, axis=1, keepdims=True)
    match_row = jnp.sum(jnp.where(eye, jnp.broadcast_to(match, (256, 256)), 0.0), axis=0, keepdims=True)
    x_send[...] = jnp.broadcast_to(match_row, (8, 256))
    xs = [send(x_send, x_recv.at[k - 1], x_s.at[k - 1], x_r.at[k - 1], across(k)) for k in (2, 1, 3)]
    gate_out[...] = (proj * gate_co[...]).astype(BF16)
    up_out[...] = (proj * up_co[...]).astype(BF16)
    outgoing = [pltpu.make_async_copy(gate_out, gate_hbm_out, out_s.at[0]), pltpu.make_async_copy(up_out, up_hbm_out, out_s.at[1])]
    for copy in outgoing:
        copy.start()

    for copy in r3s:
        copy.wait_recv()
    total = (u_own[zdiv] + r3_recv[0] + (r3_recv[1] + r3_recv[2])) * (1.0 / math.sqrt(49152))
    turned = pltpu.roll(total, 20, 0)
    f_send[...] = jnp.where(first, turned, total)[0:24]
    final = send(f_send, f_recv, pair_s.at[1], pair_r.at[1], at(dc=1))
    keep = jnp.where(first, total, turned)[0:24]
    final.wait_recv()
    got = f_recv[...]
    down_out[:, 0:128] = jnp.where(first, keep, got)[0:20]
    down_out[:, 128:256] = jnp.where(first, got, keep)[0:20]
    outgoing.append(pltpu.make_async_copy(down_out, down_hbm_out, out_s.at[2]))
    outgoing[-1].start()

    for copy in xs:
        copy.wait_recv()
    everyone = x_send[...] + x_recv[0] + (x_recv[1] + x_recv[2])
    route_out[...] = everyone[0:1] * live_row
    outgoing.append(pltpu.make_async_copy(route_out, route_hbm_out, out_s.at[3]))
    outgoing[-1].start()
    waiting = [pair, final] + fwds + psums + r3s + xs
    for group in (fars, ys, nears, r1s, r2s):
        waiting += [group[key] for key in group]
    for copy in waiting:
        copy.wait_send()
    for copy in outgoing:
        copy.wait()


def hand_over(a_in, b_in, c_in, d_in, a_out, b_out, c_out, d_out, a_mid, b_mid, c_mid, d_mid, sem_in, sem_out):
    first = [
        pltpu.make_async_copy(src, dst, sem_in.at[k])
        for k, (src, dst) in enumerate(((a_in, a_mid), (b_in, b_mid), (c_in, c_mid), (d_in, d_mid)))
    ]
    second = [
        pltpu.make_async_copy(src, dst, sem_out.at[k])
        for k, (src, dst) in enumerate(((a_mid, a_out), (b_mid, b_out), (c_mid, c_out), (d_mid, d_out)))
    ]
    for copy in first:
        copy.start()
    for k in range(4):
        first[k].wait()
        second[k].start()
    for copy in second:
        copy.wait()


def on_device(gate_pre, up_pre, out_grad, route_weight, counts, down_weight):
    hbm = pl.BlockSpec(memory_space=pl.ANY)
    dma = pltpu.SemaphoreType.DMA
    shapes = (
        jax.ShapeDtypeStruct((256, 256), BF16),
        jax.ShapeDtypeStruct((256, 256), BF16),
        jax.ShapeDtypeStruct((1, 256), F32),
        jax.ShapeDtypeStruct((20, 256), F32),
    )
    results = pl.pallas_call(
        kernel,
        out_shape=shapes,
        in_specs=[hbm] * 6,
        out_specs=(hbm, hbm, hbm, hbm),
        scratch_shapes=[
            pltpu.VMEM((256, 256), BF16),
            pltpu.VMEM((256, 256), BF16),
            pltpu.VMEM((1, 256), F32),
            pltpu.VMEM((20, 256), F32),
            pltpu.VMEM((256, 256), BF16),
            pltpu.VMEM((256, 256), BF16),
            pltpu.VMEM((256, 3840), BF16),
            pltpu.VMEM((1, 256), F32),
            pltpu.VMEM((1, 1), jnp.int32),
            pltpu.VMEM((20, 256), BF16),
            pltpu.VMEM((40, 256), F32),
            pltpu.VMEM((24, 128), F32),
            pltpu.VMEM((40, 128), F32),
            pltpu.VMEM((8, 4, 48, 128), BF16),
            pltpu.VMEM((2, 3, 8, 160, 128), BF16),
            pltpu.VMEM((3, 8, 160, 128), F32),
            pltpu.VMEM((3, 8, 160, 128), F32),
            pltpu.VMEM((3, 8, 160, 128), BF16),
            pltpu.VMEM((3, 8, 160, 128), BF16),
            pltpu.VMEM((2, 8, 160, 128), BF16),
            pltpu.VMEM((2, 8, 160, 128), BF16),
            pltpu.VMEM((160, 128), F32),
            pltpu.VMEM((7, 160, 128), BF16),
            pltpu.VMEM((7, 160, 128), BF16),
            pltpu.VMEM((4, 40, 128), F32),
            pltpu.VMEM((3, 40, 128), F32),
            pltpu.VMEM((24, 128), F32),
            pltpu.VMEM((24, 128), F32),
            pltpu.VMEM((8, 256), F32),
            pltpu.VMEM((3, 8, 256), F32),
            pltpu.VMEM((256, 256), BF16),
            pltpu.VMEM((256, 256), F32),
            pltpu.VMEM((256, 256), F32),
            dma((6,)), dma((4,)), dma((2,)), dma((2,)), dma((3,)), dma((3,)), dma((4, 8)), dma((4, 8)),
            dma((2, 8)), dma((2, 8)), dma((24,)), dma((24,)), dma((3,)), dma((3,)), dma((2, 8)), dma((2, 8)),
            dma((7,)), dma((7,)), dma((3,)), dma((3,)), dma((3,)), dma((3,)),
        ],
        compiler_params=pltpu.CompilerParams(
            collective_id=0, has_side_effects=True, vmem_limit_bytes=48 * 1024 * 1024
        ),
        cost_estimate=pl.CostEstimate(flops=1_006_632_960, bytes_accessed=3_000_000, transcendentals=65536),
    )(gate_pre, up_pre, out_grad, route_weight.reshape(1, 256), counts.reshape(1, 1), down_weight)
    gate_grad, up_grad, route_grad, down_grad = pl.pallas_call(
        hand_over,
        out_shape=shapes,
        in_specs=[hbm] * 4,
        out_specs=(hbm, hbm, hbm, hbm),
        scratch_shapes=[
            pltpu.VMEM((256, 256), BF16),
            pltpu.VMEM((256, 256), BF16),
            pltpu.VMEM((1, 256), F32),
            pltpu.VMEM((20, 256), F32),
            dma((4,)),
            dma((4,)),
        ],
        compiler_params=pltpu.CompilerParams(vmem_limit_bytes=48 * 1024 * 1024),
    )(*results)
    return (gate_grad, up_grad, route_grad.reshape(256), down_grad)


def solution(mesh):
    return jax.shard_map(
        on_device,
        mesh=mesh,
        in_specs=(
            P("dp", "expert"),
            P("dp", "expert"),
            P("dp", None),
            P("dp"),
            P("dp"),
            P("dp", "expert"),
        ),
        out_specs=(P("dp", "expert"), P("dp", "expert"), P("dp"), P("dp", "expert")),
        check_vma=False,
    )
```

```python
import math

import jax
import jax.numpy as jnp
from jax import lax
from jax.experimental import pallas as pl
from jax.experimental.pallas import tpu as pltpu
from jax.sharding import PartitionSpec as P

MESH = pl.DeviceIdType.MESH
F32, BF16 = jnp.float32, jnp.bfloat16


NEAR_FIRST = (0, 1, 7, 2, 6, 3, 5, 4)
FAR_FIRST = (4, 3, 5, 2, 6, 1, 7, 0)


def kernel(
    gate_hbm, up_hbm, og_hbm, weight_hbm, counts_hbm, w_hbm,
    gate_hbm_out, up_hbm_out, route_hbm_out, down_hbm_out,
    gate_out, up_out, route_out, down_out,
    gate_ref, up_ref, og_ref, weight_ref, counts_ref, w_ref,
    wf, g0_send, g0_recv, yb, wt, p_own, p_other, p_send, p_recv, r1_send, r1_recv,
    t_own, r2_send, r2_recv, u_own, r3_recv, f_send, f_recv, x_send, x_recv,
    hid, gate_co, up_co,
    in_s, out_s, pair_s, pair_r, far_s, far_r, y_s, y_r, near_s, near_r, fwd_s, fwd_r,
    psum_s, psum_r, r1_s, r1_r, r2_s, r2_r, r3_s, r3_r, x_s, x_r,
):
    me, x = lax.axis_index("dp"), lax.axis_index("expert")
    z, y, c = me // 16, lax.rem(me // 2, 8), lax.rem(me, 2)
    zdiv, zmod = z // 3, lax.rem(z, 3)
    first = c == 0

    def at(dz=0, dy=0, dc=0):
        return {"dp": lax.rem(z + dz, 12) * 16 + lax.rem(y + dy, 8) * 2 + lax.rem(c + dc, 2)}

    def across(k):
        return {"expert": lax.rem(x + k, 4)}

    def send(src, dst, ssem, rsem, device):
        copy = pltpu.make_async_remote_copy(
            src_ref=src, dst_ref=dst, send_sem=ssem, recv_sem=rsem, device_id=device, device_id_type=MESH
        )
        copy.start()
        return copy

    incoming = []
    for k, (src, dst) in enumerate((
        (w_hbm, w_ref), (counts_hbm, counts_ref), (weight_hbm, weight_ref),
        (gate_hbm, gate_ref), (up_hbm, up_ref), (og_hbm, og_ref),
    )):
        incoming.append(pltpu.make_async_copy(src, dst, in_s.at[k]))
        incoming[-1].start()
    barrier = pltpu.get_barrier_semaphore()
    partners = [at(dz=d) for d in (6, 3, 9)] + [at(dy=d) for d in (4, 3, 5, 2, 6, 1, 7)]
    partners += [at(dz=1), at(dz=11), at(dc=1)] + [across(k) for k in (2, 1, 3)]
    for device in partners:
        pl.semaphore_signal(barrier, inc=1, device_id=device, device_id_type=MESH)

    wf[...] = jnp.zeros_like(wf)
    g0_recv[24:40, :] = jnp.zeros((16, 128), F32)
    incoming[0].wait()
    wf[0:20, :] = w_ref[...].astype(F32)
    g0_send[...] = jnp.where(first, wf[0:24, 128:256], wf[0:24, 0:128])

    for k in range(1, 5):
        incoming[k].wait()
    eye = lax.broadcasted_iota(jnp.int32, (256, 256), 0) == lax.broadcasted_iota(jnp.int32, (256, 256), 1)
    live_row = (lax.broadcasted_iota(jnp.int32, (1, 256), 1) < counts_ref[...]).astype(F32)
    scale_row = weight_ref[...] * live_row
    scale = jnp.sum(jnp.where(eye, jnp.broadcast_to(scale_row, (256, 256)), 0.0), axis=1, keepdims=True)
    gate, up = gate_ref[...].astype(F32), up_ref[...].astype(F32)
    sig = jax.nn.sigmoid(gate)
    act = gate * sig
    hid[...] = (act * up).astype(BF16)
    gate_co[...] = scale * up * sig * (1.0 + gate * (1.0 - sig))
    up_co[...] = scale * act
    incoming[5].wait()

    def shares(ks):
        for k in ks:
            scaled = (og_ref[:, 640 * k : 640 * (k + 1)].astype(F32) * scale).astype(BF16)
            part = lax.dot_general(scaled, hid[...], (((0,), (0,)), ((), ())), preferred_element_type=F32)
            lo, hi = part[:, 0:128], part[:, 128:256]
            own, other = jnp.where(first, lo, hi), jnp.where(first, hi, lo)
            for b in (0, 1):
                m, j = (2 * k + b) % 3, (2 * k + b) // 3
                for i in range(8):
                    at_row = 320 * b + 40 * i
                    p_own[m, i, 40 * j : 40 * j + 40, :] = own[at_row : at_row + 40]
                    p_other[m, i, 40 * j : 40 * j + 40, :] = other[at_row : at_row + 40]

    shares(range(6))
    pl.semaphore_wait(barrier, len(partners))
    pair = send(g0_send, g0_recv.at[pl.ds(0, 24)], pair_s.at[0], pair_r.at[0], at(dc=1))
    pair.wait_recv()
    mine = jnp.where(first, wf[:, 0:128], wf[:, 128:256])
    other = g0_recv[...]
    block = jnp.where(first, mine + pltpu.roll(other, 20, 0), other + pltpu.roll(mine, 20, 0))
    yb[y, zdiv] = jnp.concatenate([block, jnp.zeros((8, 128), F32)], axis=0).astype(BF16)
    piece = yb.at[y, zdiv]
    fars = {k: send(piece, piece, far_s.at[k - 1], far_r.at[k - 1], at(dz=3 * k)) for k in (2, 1, 3)}
    ys = {}

    def along_y(k):
        piece = yb.at[y, lax.rem(zdiv + 4 - k, 4)]
        for d in NEAR_FIRST[1:]:
            ys[k, d] = send(piece, piece, y_s.at[k, d], y_r.at[k, d], at(dy=d))

    along_y(0)

    psums = []
    for k in (1, 2, 0):
        m = lax.rem(zmod + k, 3)
        p_send[m] = p_other[m].astype(BF16)
        psums.append(send(p_send.at[m], p_recv.at[m], psum_s.at[k], psum_r.at[k], at(dc=1)))

    r1s = {}
    psums[0].wait_recv()
    psums[1].wait_recv()
    for d in FAR_FIRST:
        i = lax.rem(y + d, 8)
        for side, step in enumerate((1, 11)):
            m = lax.rem(zmod + step, 3)
            r1_send[side, i] = (p_own[m, i] + p_recv[m, i].astype(F32)).astype(BF16)
            r1s[side, d] = send(
                r1_send.at[side, i], r1_recv.at[side, i], r1_s.at[side, d], r1_r.at[side, d], at(dz=step)
            )

    for k in (1, 3, 2):
        fars[k].wait_recv()
        along_y(k)
    nears, fwds = {}, []

    def forward(m, i, sem):
        piece = wt.at[c, m, i]
        fwds.append(send(piece, piece, fwd_s.at[sem], fwd_r.at[sem], at(dc=1)))

    psums[2].wait_recv()
    r2s = {}
    for n in range(8):
        d = NEAR_FIRST[n]
        if d:
            for k in range(4):
                ys[k, d].wait_recv()
        i = lax.rem(y + 8 - d, 8)
        wt[c, zmod, i] = jnp.concatenate([yb[i, j].astype(F32)[0:40] for j in range(4)], axis=0).astype(BF16)
        for side, step in enumerate((1, 11)):
            piece = wt.at[c, zmod, i]
            nears[side, d] = send(piece, piece, near_s.at[side, d], near_r.at[side, d], at(dz=step))
        forward(zmod, i, d)
        d = FAR_FIRST[n]
        r1s[0, d].wait_recv()
        r1s[1, d].wait_recv()
        i = lax.rem(y + d, 8)
        total = p_own[zmod, i] + p_recv[zmod, i].astype(F32)
        total = total + (r1_recv[0, i].astype(F32) + r1_recv[1, i].astype(F32))
        if d:
            r2_send[d - 1] = total.astype(BF16)
            r2s[d] = send(r2_send.at[d - 1], r2_recv.at[d - 1], r2_s.at[d - 1], r2_r.at[d - 1], at(dy=d))
        else:
            t_own[...] = total

    for n in range(8):
        d = NEAR_FIRST[n]
        i = lax.rem(y + 8 - d, 8)
        for side in range(2):
            nears[side, d].wait_recv()
            forward(lax.rem(zmod + 2 - side, 3), i, 8 * side + 8 + d)

    total = t_own[...]
    for d in NEAR_FIRST[1:]:
        r2s[d].wait_recv()
        total = total + r2_recv[d - 1].astype(F32)
    u_own[...] = total.reshape(4, 40, 128)
    r3s = [
        send(u_own.at[lax.rem(zdiv + k, 4)], r3_recv.at[k - 1], r3_s.at[k - 1], r3_r.at[k - 1], at(dz=3 * k))
        for k in (2, 1, 3)
    ]

    for copy in fwds:
        copy.wait_recv()
    proj = None
    for k in range(6):
        halves = []
        for h in range(2):
            rows = [
                wt[h, b % 3, i].astype(F32)[40 * (b // 3) : 40 * (b // 3) + 40] for b in (2 * k, 2 * k + 1) for i in range(8)
            ]
            halves.append(jnp.concatenate(rows, axis=0).astype(BF16))
        term = jnp.dot(
            og_ref[:, 640 * k : 640 * (k + 1)], jnp.concatenate(halves, axis=1), preferred_element_type=F32
        )
        proj = term if proj is None else proj + term
    match = jnp.sum(hid[...].astype(F32) * proj, axis=1, keepdims=True)
    match_row = jnp.sum(jnp.where(eye, jnp.broadcast_to(match, (256, 256)), 0.0), axis=0, keepdims=True)
    x_send[...] = jnp.broadcast_to(match_row, (8, 256))
    xs = [send(x_send, x_recv.at[k - 1], x_s.at[k - 1], x_r.at[k - 1], across(k)) for k in (2, 1, 3)]
    gate_out[...] = (proj * gate_co[...]).astype(BF16)
    up_out[...] = (proj * up_co[...]).astype(BF16)
    outgoing = [pltpu.make_async_copy(gate_out, gate_hbm_out, out_s.at[0]), pltpu.make_async_copy(up_out, up_hbm_out, out_s.at[1])]
    for copy in outgoing:
        copy.start()

    for copy in r3s:
        copy.wait_recv()
    total = (u_own[zdiv] + r3_recv[0] + (r3_recv[1] + r3_recv[2])) * (1.0 / math.sqrt(49152))
    turned = pltpu.roll(total, 20, 0)
    f_send[...] = jnp.where(first, turned, total)[0:24]
    final = send(f_send, f_recv, pair_s.at[1], pair_r.at[1], at(dc=1))
    keep = jnp.where(first, total, turned)[0:24]
    final.wait_recv()
    got = f_recv[...]
    down_out[:, 0:128] = jnp.where(first, keep, got)[0:20]
    down_out[:, 128:256] = jnp.where(first, got, keep)[0:20]
    outgoing.append(pltpu.make_async_copy(down_out, down_hbm_out, out_s.at[2]))
    outgoing[-1].start()

    for copy in xs:
        copy.wait_recv()
    everyone = x_send[...] + x_recv[0] + (x_recv[1] + x_recv[2])
    route_out[...] = everyone[0:1] * live_row
    outgoing.append(pltpu.make_async_copy(route_out, route_hbm_out, out_s.at[3]))
    outgoing[-1].start()
    waiting = [pair, final] + fwds + psums + r3s + xs
    for group in (fars, ys, nears, r1s, r2s):
        waiting += [group[key] for key in group]
    for copy in waiting:
        copy.wait_send()
    for copy in outgoing:
        copy.wait()


def hand_over(a_in, b_in, c_in, d_in, a_out, b_out, c_out, d_out, a_mid, b_mid, c_mid, d_mid, sem_in, sem_out):
    first = [
        pltpu.make_async_copy(src, dst, sem_in.at[k])
        for k, (src, dst) in enumerate(((a_in, a_mid), (b_in, b_mid), (c_in, c_mid), (d_in, d_mid)))
    ]
    second = [
        pltpu.make_async_copy(src, dst, sem_out.at[k])
        for k, (src, dst) in enumerate(((a_mid, a_out), (b_mid, b_out), (c_mid, c_out), (d_mid, d_out)))
    ]
    for copy in first:
        copy.start()
    for k in range(4):
        first[k].wait()
        second[k].start()
    for copy in second:
        copy.wait()


def on_device(gate_pre, up_pre, out_grad, route_weight, counts, down_weight):
    hbm = pl.BlockSpec(memory_space=pl.ANY)
    dma = pltpu.SemaphoreType.DMA
    shapes = (
        jax.ShapeDtypeStruct((256, 256), BF16),
        jax.ShapeDtypeStruct((256, 256), BF16),
        jax.ShapeDtypeStruct((1, 256), F32),
        jax.ShapeDtypeStruct((20, 256), F32),
    )
    results = pl.pallas_call(
        kernel,
        out_shape=shapes,
        in_specs=[hbm] * 6,
        out_specs=(hbm, hbm, hbm, hbm),
        scratch_shapes=[
            pltpu.VMEM((256, 256), BF16),
            pltpu.VMEM((256, 256), BF16),
            pltpu.VMEM((1, 256), F32),
            pltpu.VMEM((20, 256), F32),
            pltpu.VMEM((256, 256), BF16),
            pltpu.VMEM((256, 256), BF16),
            pltpu.VMEM((256, 3840), BF16),
            pltpu.VMEM((1, 256), F32),
            pltpu.VMEM((1, 1), jnp.int32),
            pltpu.VMEM((20, 256), BF16),
            pltpu.VMEM((40, 256), F32),
            pltpu.VMEM((24, 128), F32),
            pltpu.VMEM((40, 128), F32),
            pltpu.VMEM((8, 4, 48, 128), BF16),
            pltpu.VMEM((2, 3, 8, 160, 128), BF16),
            pltpu.VMEM((3, 8, 160, 128), F32),
            pltpu.VMEM((3, 8, 160, 128), F32),
            pltpu.VMEM((3, 8, 160, 128), BF16),
            pltpu.VMEM((3, 8, 160, 128), BF16),
            pltpu.VMEM((2, 8, 160, 128), BF16),
            pltpu.VMEM((2, 8, 160, 128), BF16),
            pltpu.VMEM((160, 128), F32),
            pltpu.VMEM((7, 160, 128), BF16),
            pltpu.VMEM((7, 160, 128), BF16),
            pltpu.VMEM((4, 40, 128), F32),
            pltpu.VMEM((3, 40, 128), F32),
            pltpu.VMEM((24, 128), F32),
            pltpu.VMEM((24, 128), F32),
            pltpu.VMEM((8, 256), F32),
            pltpu.VMEM((3, 8, 256), F32),
            pltpu.VMEM((256, 256), BF16),
            pltpu.VMEM((256, 256), F32),
            pltpu.VMEM((256, 256), F32),
            dma((6,)), dma((4,)), dma((2,)), dma((2,)), dma((3,)), dma((3,)), dma((4, 8)), dma((4, 8)),
            dma((2, 8)), dma((2, 8)), dma((24,)), dma((24,)), dma((3,)), dma((3,)), dma((2, 8)), dma((2, 8)),
            dma((7,)), dma((7,)), dma((3,)), dma((3,)), dma((3,)), dma((3,)),
        ],
        compiler_params=pltpu.CompilerParams(
            collective_id=0, has_side_effects=True, vmem_limit_bytes=56 * 1024 * 1024
        ),
        cost_estimate=pl.CostEstimate(flops=1_006_632_960, bytes_accessed=3_000_000, transcendentals=65536),
    )(gate_pre, up_pre, out_grad, route_weight.reshape(1, 256), counts.reshape(1, 1), down_weight)
    gate_grad, up_grad, route_grad, down_grad = pl.pallas_call(
        hand_over,
        out_shape=shapes,
        in_specs=[hbm] * 4,
        out_specs=(hbm, hbm, hbm, hbm),
        scratch_shapes=[
            pltpu.VMEM((256, 256), BF16),
            pltpu.VMEM((256, 256), BF16),
            pltpu.VMEM((1, 256), F32),
            pltpu.VMEM((20, 256), F32),
            dma((4,)),
            dma((4,)),
        ],
        compiler_params=pltpu.CompilerParams(vmem_limit_bytes=56 * 1024 * 1024),
    )(*results)
    return (gate_grad, up_grad, route_grad.reshape(256), down_grad)


def solution(mesh):
    return jax.shard_map(
        on_device,
        mesh=mesh,
        in_specs=(
            P("dp", "expert"),
            P("dp", "expert"),
            P("dp", None),
            P("dp"),
            P("dp"),
            P("dp", "expert"),
        ),
        out_specs=(P("dp", "expert"), P("dp", "expert"), P("dp"), P("dp", "expert")),
        check_vma=False,
    )
```

```python
import math

import jax
import jax.numpy as jnp
from jax import lax
from jax.experimental import pallas as pl
from jax.experimental.pallas import tpu as pltpu
from jax.sharding import PartitionSpec as P

MESH = pl.DeviceIdType.MESH
F32, BF16 = jnp.float32, jnp.bfloat16


NEAR_FIRST = (0, 1, 7, 2, 6, 3, 5, 4)
SUM_ORDER = (2, 6, 4, 3, 5, 1, 7, 0)
GROUPS = ((0, 3), (3, 2), (5, 3))


def kernel(
    gate_hbm, up_hbm, og_hbm, weight_hbm, counts_hbm, w_hbm,
    gate_hbm_out, up_hbm_out, route_hbm_out, down_hbm_out,
    gate_out, up_out, route_out, down_out,
    gate_ref, up_ref, og_ref, weight_ref, counts_ref, w_ref,
    wf, g0_send, g0_recv, yb, wt, p_own, p_other, p_send, p_recv, r1_send, r1_recv,
    t_own, r2_send, r2_recv, u_own, r3_recv, f_send, f_recv, x_send, x_recv,
    hid, gate_co, up_co, wn,
    in_s, out_s, pair_s, pair_r, far_s, far_r, y_s, y_r, near_s, near_r, fwd_s, fwd_r,
    psum_s, psum_r, r1_s, r1_r, r2_s, r2_r, r3_s, r3_r, x_s, x_r,
):
    me, x = lax.axis_index("dp"), lax.axis_index("expert")
    z, y, c = me // 16, lax.rem(me // 2, 8), lax.rem(me, 2)
    zdiv, zmod = z // 3, lax.rem(z, 3)
    first = c == 0

    def at(dz=0, dy=0, dc=0):
        return {"dp": lax.rem(z + dz, 12) * 16 + lax.rem(y + dy, 8) * 2 + lax.rem(c + dc, 2)}

    def across(k):
        return {"expert": lax.rem(x + k, 4)}

    def send(src, dst, ssem, rsem, device):
        copy = pltpu.make_async_remote_copy(
            src_ref=src, dst_ref=dst, send_sem=ssem, recv_sem=rsem, device_id=device, device_id_type=MESH
        )
        copy.start()
        return copy

    incoming = []
    for k, (src, dst) in enumerate((
        (w_hbm, w_ref), (counts_hbm, counts_ref), (weight_hbm, weight_ref),
        (gate_hbm, gate_ref), (up_hbm, up_ref), (og_hbm, og_ref),
    )):
        incoming.append(pltpu.make_async_copy(src, dst, in_s.at[k]))
        incoming[-1].start()
    barrier = pltpu.get_barrier_semaphore()
    partners = [at(dz=d) for d in (6, 3, 9)] + [at(dy=d) for d in (4, 3, 5, 2, 6, 1, 7)]
    partners += [at(dz=1), at(dz=11), at(dc=1)] + [across(k) for k in (2, 1, 3)]
    for device in partners:
        pl.semaphore_signal(barrier, inc=1, device_id=device, device_id_type=MESH)

    wf[...] = jnp.zeros_like(wf)
    g0_recv[24:40, :] = jnp.zeros((16, 128), F32)
    incoming[0].wait()
    wf[0:20, :] = w_ref[...].astype(F32)
    g0_send[...] = jnp.where(first, wf[0:24, 128:256], wf[0:24, 0:128])

    for k in range(1, 5):
        incoming[k].wait()
    eye = lax.broadcasted_iota(jnp.int32, (256, 256), 0) == lax.broadcasted_iota(jnp.int32, (256, 256), 1)
    live_row = (lax.broadcasted_iota(jnp.int32, (1, 256), 1) < counts_ref[...]).astype(F32)
    scale_row = weight_ref[...] * live_row
    scale = jnp.sum(jnp.where(eye, jnp.broadcast_to(scale_row, (256, 256)), 0.0), axis=1, keepdims=True)
    gate, up = gate_ref[...].astype(F32), up_ref[...].astype(F32)
    sig = jax.nn.sigmoid(gate)
    act = gate * sig
    hid[...] = (act * up).astype(BF16)
    gate_co[...] = scale * up * sig * (1.0 + gate * (1.0 - sig))
    up_co[...] = scale * act
    incoming[5].wait()

    def shares(ks):
        for k in ks:
            scaled = (og_ref[:, 640 * k : 640 * (k + 1)].astype(F32) * scale).astype(BF16)
            part = lax.dot_general(scaled, hid[...], (((0,), (0,)), ((), ())), preferred_element_type=F32)
            lo, hi = part[:, 0:128], part[:, 128:256]
            own, other = jnp.where(first, lo, hi), jnp.where(first, hi, lo)
            for b in (0, 1):
                m, j = (2 * k + b) % 3, (2 * k + b) // 3
                for i in range(8):
                    at_row = 320 * b + 40 * i
                    p_own[m, i, 40 * j : 40 * j + 40, :] = own[at_row : at_row + 40]
                    p_other[m, i, 40 * j : 40 * j + 40, :] = other[at_row : at_row + 40]

    shares(range(6))
    for m in range(3):
        p_send[m] = p_other[m].astype(BF16)
    pl.semaphore_wait(barrier, len(partners))
    pair = send(g0_send, g0_recv.at[pl.ds(0, 24)], pair_s.at[0], pair_r.at[0], at(dc=1))
    psums = []
    for k in (1, 2, 0):
        m = lax.rem(zmod + k, 3)
        psums.append(send(p_send.at[m], p_recv.at[m], psum_s.at[k], psum_r.at[k], at(dc=1)))

    pair.wait_recv()
    mine = jnp.where(first, wf[:, 0:128], wf[:, 128:256])
    other = g0_recv[...]
    block = jnp.where(first, mine + pltpu.roll(other, 20, 0), other + pltpu.roll(mine, 20, 0))
    def z_slot(k):
        return k + (k // 2) * (1 - 2 * (k // 3))

    def y_slot(d):
        return (1 - d // 5) * (2 * d - 1) + (d // 5) * (16 - 2 * d) + (7 - d) // 7

    yb[0, 0] = jnp.concatenate([block, jnp.zeros((8, 128), F32)], axis=0).astype(BF16)
    fars = {
        k: send(yb.at[0, 0], yb.at[0, z_slot(k)], far_s.at[k - 1], far_r.at[k - 1], at(dz=3 * k)) for k in (2, 1, 3)
    }
    ys = {}

    def along_y(part, slots):
        for d in NEAR_FIRST[1:]:
            ys[part, d] = send(
                yb.at[0, slots], yb.at[y_slot(d), slots], y_s.at[part, d], y_r.at[part, d], at(dy=d)
            )

    along_y(0, pl.ds(0, 1))

    r1s = {}
    psums[0].wait_recv()
    psums[1].wait_recv()
    for g, (start, size) in enumerate(GROUPS):
        for side, step in enumerate((1, 11)):
            m = lax.rem(zmod + step, 3)
            for n in range(start, start + size):
                i = lax.rem(y + SUM_ORDER[n], 8)
                r1_send[side, n] = (p_own[m, i] + p_recv[m, i].astype(F32)).astype(BF16)
            span = pl.ds(start, size)
            r1s[side, g] = send(
                r1_send.at[side, span], r1_recv.at[side, span], r1_s.at[side, g], r1_r.at[side, g], at(dz=step)
            )

    fars[1].wait_recv()
    fars[3].wait_recv()
    along_y(1, pl.ds(1, 2))
    fars[2].wait_recv()
    along_y(2, pl.ds(3, 1))
    nears, fwds = {}, []

    def forward(m, g, sem):
        piece = wt.at[c, m, pl.ds(GROUPS[g][0], GROUPS[g][1])]
        fwds.append(send(piece, piece, fwd_s.at[sem], fwd_r.at[sem], at(dc=1)))

    psums[2].wait_recv()
    r2s = {}
    z_slots = [z_slot(lax.rem(zdiv + 4 - j, 4)) for j in range(4)]
    for g, (start, size) in enumerate(GROUPS):
        for n in range(start, start + size):
            d = NEAR_FIRST[n]
            if d:
                for part in range(3):
                    ys[part, d].wait_recv()
            rows = [yb[n, z_slots[j]].astype(F32)[0:40] for j in range(4)]
            wt[c, zmod, n] = jnp.concatenate(rows, axis=0).astype(BF16)
        piece = wt.at[c, zmod, pl.ds(start, size)]
        for side, step in enumerate((1, 11)):
            nears[side, g] = send(piece, piece, near_s.at[side, g], near_r.at[side, g], at(dz=step))
        forward(zmod, g, g)
        r1s[0, g].wait_recv()
        r1s[1, g].wait_recv()
        for n in range(start, start + size):
            d = SUM_ORDER[n]
            i = lax.rem(y + d, 8)
            total = p_own[zmod, i] + p_recv[zmod, i].astype(F32)
            total = total + (r1_recv[0, n].astype(F32) + r1_recv[1, n].astype(F32))
            if d:
                r2_send[d - 1] = total.astype(BF16)
                r2s[d] = send(r2_send.at[d - 1], r2_recv.at[d - 1], r2_s.at[d - 1], r2_r.at[d - 1], at(dy=d))
            else:
                t_own[...] = total

    def settle(h, m):
        for j in range(4):
            rows = [wt[h, m, y_slots[i]].astype(F32)[40 * j : 40 * j + 40] for i in range(8)]
            wn[h, 3 * j + m] = jnp.concatenate(rows, axis=0).astype(BF16)

    y_slots = [y_slot(lax.rem(y + 8 - i, 8)) for i in range(8)]
    settle(c, zmod)
    for copy in fwds[:3]:
        copy.wait_recv()
    settle(1 - c, zmod)
    for g in range(3):
        for side in range(2):
            nears[side, g].wait_recv()
            forward(lax.rem(zmod + 2 - side, 3), g, 3 * side + 3 + g)
    for side in range(2):
        settle(c, lax.rem(zmod + 2 - side, 3))

    total = t_own[...]
    for d in NEAR_FIRST[1:]:
        r2s[d].wait_recv()
        total = total + r2_recv[d - 1].astype(F32)
    u_own[...] = total.reshape(4, 40, 128)
    r3s = [
        send(u_own.at[lax.rem(zdiv + k, 4)], r3_recv.at[k - 1], r3_s.at[k - 1], r3_r.at[k - 1], at(dz=3 * k))
        for k in (2, 1, 3)
    ]

    for copy in fwds[3:]:
        copy.wait_recv()
    for side in range(2):
        settle(1 - c, lax.rem(zmod + 2 - side, 3))
    proj = None
    for k in range(6):
        both = jnp.concatenate([wn[h, 2 * k : 2 * k + 2].reshape(640, 128) for h in range(2)], axis=1)
        term = jnp.dot(og_ref[:, 640 * k : 640 * (k + 1)], both, preferred_element_type=F32)
        proj = term if proj is None else proj + term
    match = jnp.sum(hid[...].astype(F32) * proj, axis=1, keepdims=True)
    match_row = jnp.sum(jnp.where(eye, jnp.broadcast_to(match, (256, 256)), 0.0), axis=0, keepdims=True)
    x_send[...] = jnp.broadcast_to(match_row, (8, 256))
    xs = [send(x_send, x_recv.at[k - 1], x_s.at[k - 1], x_r.at[k - 1], across(k)) for k in (2, 1, 3)]
    gate_out[...] = (proj * gate_co[...]).astype(BF16)
    up_out[...] = (proj * up_co[...]).astype(BF16)
    outgoing = [pltpu.make_async_copy(gate_out, gate_hbm_out, out_s.at[0]), pltpu.make_async_copy(up_out, up_hbm_out, out_s.at[1])]
    for copy in outgoing:
        copy.start()

    for copy in r3s:
        copy.wait_recv()
    total = (u_own[zdiv] + r3_recv[0] + (r3_recv[1] + r3_recv[2])) * (1.0 / math.sqrt(49152))
    turned = pltpu.roll(total, 20, 0)
    f_send[...] = jnp.where(first, turned, total)[0:24]
    final = send(f_send, f_recv, pair_s.at[1], pair_r.at[1], at(dc=1))
    keep = jnp.where(first, total, turned)[0:24]
    final.wait_recv()
    got = f_recv[...]
    down_out[:, 0:128] = jnp.where(first, keep, got)[0:20]
    down_out[:, 128:256] = jnp.where(first, got, keep)[0:20]
    outgoing.append(pltpu.make_async_copy(down_out, down_hbm_out, out_s.at[2]))
    outgoing[-1].start()

    for copy in xs:
        copy.wait_recv()
    everyone = x_send[...] + x_recv[0] + (x_recv[1] + x_recv[2])
    route_out[...] = everyone[0:1] * live_row
    outgoing.append(pltpu.make_async_copy(route_out, route_hbm_out, out_s.at[3]))
    outgoing[-1].start()
    waiting = [pair, final] + fwds + psums + r3s + xs
    for group in (fars, ys, nears, r1s, r2s):
        waiting += [group[key] for key in group]
    for copy in waiting:
        copy.wait_send()
    for copy in outgoing:
        copy.wait()


def hand_over(a_in, b_in, c_in, d_in, a_out, b_out, c_out, d_out, a_mid, b_mid, c_mid, d_mid, sem_in, sem_out):
    first = [
        pltpu.make_async_copy(src, dst, sem_in.at[k])
        for k, (src, dst) in enumerate(((a_in, a_mid), (b_in, b_mid), (c_in, c_mid), (d_in, d_mid)))
    ]
    second = [
        pltpu.make_async_copy(src, dst, sem_out.at[k])
        for k, (src, dst) in enumerate(((a_mid, a_out), (b_mid, b_out), (c_mid, c_out), (d_mid, d_out)))
    ]
    for copy in first:
        copy.start()
    for k in range(4):
        first[k].wait()
        second[k].start()
    for copy in second:
        copy.wait()


def on_device(gate_pre, up_pre, out_grad, route_weight, counts, down_weight):
    hbm = pl.BlockSpec(memory_space=pl.ANY)
    dma = pltpu.SemaphoreType.DMA
    shapes = (
        jax.ShapeDtypeStruct((256, 256), BF16),
        jax.ShapeDtypeStruct((256, 256), BF16),
        jax.ShapeDtypeStruct((1, 256), F32),
        jax.ShapeDtypeStruct((20, 256), F32),
    )
    results = pl.pallas_call(
        kernel,
        out_shape=shapes,
        in_specs=[hbm] * 6,
        out_specs=(hbm, hbm, hbm, hbm),
        scratch_shapes=[
            pltpu.VMEM((256, 256), BF16),
            pltpu.VMEM((256, 256), BF16),
            pltpu.VMEM((1, 256), F32),
            pltpu.VMEM((20, 256), F32),
            pltpu.VMEM((256, 256), BF16),
            pltpu.VMEM((256, 256), BF16),
            pltpu.VMEM((256, 3840), BF16),
            pltpu.VMEM((1, 256), F32),
            pltpu.VMEM((1, 1), jnp.int32),
            pltpu.VMEM((20, 256), BF16),
            pltpu.VMEM((40, 256), F32),
            pltpu.VMEM((24, 128), F32),
            pltpu.VMEM((40, 128), F32),
            pltpu.VMEM((8, 4, 48, 128), BF16),
            pltpu.VMEM((2, 3, 8, 160, 128), BF16),
            pltpu.VMEM((3, 8, 160, 128), F32),
            pltpu.VMEM((3, 8, 160, 128), F32),
            pltpu.VMEM((3, 8, 160, 128), BF16),
            pltpu.VMEM((3, 8, 160, 128), BF16),
            pltpu.VMEM((2, 8, 160, 128), BF16),
            pltpu.VMEM((2, 8, 160, 128), BF16),
            pltpu.VMEM((160, 128), F32),
            pltpu.VMEM((7, 160, 128), BF16),
            pltpu.VMEM((7, 160, 128), BF16),
            pltpu.VMEM((4, 40, 128), F32),
            pltpu.VMEM((3, 40, 128), F32),
            pltpu.VMEM((24, 128), F32),
            pltpu.VMEM((24, 128), F32),
            pltpu.VMEM((8, 256), F32),
            pltpu.VMEM((3, 8, 256), F32),
            pltpu.VMEM((256, 256), BF16),
            pltpu.VMEM((256, 256), F32),
            pltpu.VMEM((256, 256), F32),
            pltpu.VMEM((2, 12, 320, 128), BF16),
            dma((6,)), dma((4,)), dma((2,)), dma((2,)), dma((3,)), dma((3,)), dma((3, 8)), dma((3, 8)),
            dma((2, 3)), dma((2, 3)), dma((9,)), dma((9,)), dma((3,)), dma((3,)), dma((2, 3)), dma((2, 3)),
            dma((7,)), dma((7,)), dma((3,)), dma((3,)), dma((3,)), dma((3,)),
        ],
        compiler_params=pltpu.CompilerParams(
            collective_id=0, has_side_effects=True, vmem_limit_bytes=56 * 1024 * 1024
        ),
        cost_estimate=pl.CostEstimate(flops=1_006_632_960, bytes_accessed=3_000_000, transcendentals=65536),
    )(gate_pre, up_pre, out_grad, route_weight.reshape(1, 256), counts.reshape(1, 1), down_weight)
    gate_grad, up_grad, route_grad, down_grad = pl.pallas_call(
        hand_over,
        out_shape=shapes,
        in_specs=[hbm] * 4,
        out_specs=(hbm, hbm, hbm, hbm),
        scratch_shapes=[
            pltpu.VMEM((256, 256), BF16),
            pltpu.VMEM((256, 256), BF16),
            pltpu.VMEM((1, 256), F32),
            pltpu.VMEM((20, 256), F32),
            dma((4,)),
            dma((4,)),
        ],
        compiler_params=pltpu.CompilerParams(vmem_limit_bytes=56 * 1024 * 1024),
    )(*results)
    return (gate_grad, up_grad, route_grad.reshape(256), down_grad)


def solution(mesh):
    return jax.shard_map(
        on_device,
        mesh=mesh,
        in_specs=(
            P("dp", "expert"),
            P("dp", "expert"),
            P("dp", None),
            P("dp"),
            P("dp"),
            P("dp", "expert"),
        ),
        out_specs=(P("dp", "expert"), P("dp", "expert"), P("dp"), P("dp", "expert")),
        check_vma=False,
    )
```
